32 devices in a mesh: row: 8 (over z, core), col: 2 (over x), depth: 2 (over y).
Axes of the slice: x: 2, y: 2, z: 4, core: 2. Of those that a mesh axis runs over, the one named last changes fastest.
Arguments:
- inputs: bfloat16 [1024, 6144], P(('depth', 'col'), 'row'), may hold values from -6 to 6
- cotangent: bfloat16 [1024, 6144], P(('depth', 'col'), 'row'), may hold values from -1.5 to 1.5
- w_in: bfloat16 [6144, 24576], P('row', 'col'), may hold values from -0.078125 to 0.078125
- w_out: bfloat16 [24576, 6144], P('col', 'row'), may hold values from -0.0390625 to 0.0390625
Outputs:
- outputs: bfloat16 [1024, 6144], P(('depth', 'col'), 'row')
- grad_inputs: bfloat16 [1024, 6144], P(('depth', 'col'), 'row')
- grad_w_in: bfloat16 [6144, 24576], P('row', ('col', 'depth'))
- grad_w_out: bfloat16 [24576, 6144], P('col', ('row', 'depth'))
The draws below stay inside these ranges and needn't reach their ends.
All inputs are finite; a program needn't handle non-finite values.
Results may differ from the reference program's by a relative error of at most 0.03.
Values may be sent and summed in bfloat16 or wider, within the bound.
A program may use at most 192 MiB of HBM per device.

```python
import jax
import jax.numpy as jnp
from jax import lax

D = 6144
FF = 24576
GROUP_TOKENS = 512
TOKENS = 1024
N_ROW = 8
N_DEPTH = 2


def steps_of(key, dims, pieces, low, high):
    def one(position, parts):
        steps = jax.random.uniform(jax.random.fold_in(jax.random.fold_in(key, 6), position), (parts,), jnp.float32, low / len(pieces), high / len(pieces))
        return jnp.repeat(jnp.exp(steps), dims[position] // parts).reshape((-1,) + (1,) * (len(dims) - position - 1))

    loudness = one(*pieces[0])
    for cut in pieces[1:]:
        loudness = loudness * one(*cut)
    return loudness


def gaussian(stream_key, dims, width, limit, cuts=(), held_as=jnp.bfloat16):
    entries = width * jax.random.normal(stream_key, dims, jnp.float32)
    if cuts:
        entries = entries * steps_of(stream_key, dims, cuts, -0.22, 0.18)
    return jnp.clip(entries, -limit, limit).astype(held_as)


def setup_inputs(seed: int = 0) -> dict:
    streams_of = jax.random.split(jax.random.key(seed), 5)
    inputs = gaussian(streams_of[0], (TOKENS, D), 1.0, 6.0, ((0, 4), (1, 8)))
    cotangent = gaussian(streams_of[1], (TOKENS, D), 0.25, 1.5, ((0, 4), (1, 8)))
    w_in = gaussian(streams_of[2], (D, FF), D ** -0.5, 0.078125, ((0, 8), (1, 2)))
    w_out = gaussian(streams_of[3], (FF, D), FF ** -0.5, 0.0390625, ((0, 2), (1, 8)))
    return {"inputs": inputs, "cotangent": cotangent, "w_in": w_in, "w_out": w_out}


gelu_c = 0.7978845608028654
gelu_k = 0.044715


def gelu_pair(preact):
    inner = gelu_c * (preact + gelu_k * preact * preact * preact)
    tangent = jnp.tanh(inner)
    gelu_value = 0.5 * preact * (1.0 + tangent)
    gelu_slope = 0.5 * (1.0 + tangent) + 0.5 * preact * (1.0 - tangent * tangent) * gelu_c * (1.0 + 3.0 * gelu_k * preact * preact)
    return gelu_value, gelu_slope


def round_trip(values):
    return lax.optimization_barrier(values.astype(jnp.bfloat16)).astype(jnp.float32)


def reference(inputs, cotangent, w_in, w_out):
    blocks = D // N_ROW

    def add_pre(index, carry):
        offset = (index * blocks).astype(jnp.int32)
        left = lax.dynamic_slice_in_dim(inputs, offset, blocks, 1)
        right = lax.dynamic_slice_in_dim(w_in, offset, blocks, 0)
        return carry + round_trip(jnp.dot(left, right, preferred_element_type=jnp.float32))

    preact = lax.fori_loop(0, N_ROW, add_pre, jnp.zeros((TOKENS, FF), jnp.float32))
    gelu_value, gelu_slope = gelu_pair(preact)
    hidden = gelu_value.astype(jnp.bfloat16)
    outputs = jnp.dot(hidden, w_out, preferred_element_type=jnp.float32).astype(jnp.bfloat16)

    def add_back(index, carry):
        offset = (index * blocks).astype(jnp.int32)
        left = lax.dynamic_slice_in_dim(cotangent, offset, blocks, 1)
        right = lax.dynamic_slice_in_dim(w_out, offset, blocks, 1)
        term = lax.dot_general(left, right, (((1,), (1,)), ((), ())), preferred_element_type=jnp.float32)
        return carry + round_trip(term)

    grad_hidden = lax.fori_loop(0, N_ROW, add_back, jnp.zeros((TOKENS, FF), jnp.float32)).astype(jnp.bfloat16)
    grad_pre = (grad_hidden.astype(jnp.float32) * gelu_slope).astype(jnp.bfloat16)
    grad_inputs = lax.dot_general(grad_pre, w_in, (((1,), (1,)), ((), ())), preferred_element_type=jnp.float32).astype(jnp.bfloat16)
    grad_w_out = jnp.zeros((FF, D), jnp.float32)
    grad_w_in = jnp.zeros((D, FF), jnp.float32)
    for group in range(N_DEPTH):
        first_row = group * GROUP_TOKENS
        hidden_part = hidden[first_row:first_row + GROUP_TOKENS]
        cot_part = cotangent[first_row:first_row + GROUP_TOKENS]
        input_part = inputs[first_row:first_row + GROUP_TOKENS]
        slope_part = grad_pre[first_row:first_row + GROUP_TOKENS]
        grad_w_out = grad_w_out + round_trip(lax.dot_general(hidden_part, cot_part, (((0,), (0,)), ((), ())), preferred_element_type=jnp.float32))
        grad_w_in = grad_w_in + round_trip(lax.dot_general(input_part, slope_part, (((0,), (0,)), ((), ())), preferred_element_type=jnp.float32))
    return outputs, grad_inputs, grad_w_in.astype(jnp.bfloat16), grad_w_out.astype(jnp.bfloat16)
```

```python
import jax
import jax.numpy as jnp
from jax import lax
from jax.sharding import PartitionSpec as P

gelu_c = 0.7978845608028654
gelu_k = 0.044715


def gelu_pair(preact):
    inner = gelu_c * (preact + gelu_k * preact * preact * preact)
    tangent = jnp.tanh(inner)
    gelu_value = 0.5 * preact * (1.0 + tangent)
    gelu_slope = 0.5 * (1.0 + tangent) + 0.5 * preact * (1.0 - tangent * tangent) * gelu_c * (
        1.0 + 3.0 * gelu_k * preact * preact
    )
    return (gelu_value, gelu_slope)


CHUNKS = 2


def on_device(n_depth, inputs, cotangent, w_in, w_out):
    depth = lax.axis_index("depth")
    units = w_in.shape[1] // n_depth
    x_all = lax.all_gather(inputs, ("depth", "col"), axis=0, tiled=True)
    dy_all = lax.all_gather(cotangent, ("depth", "col"), axis=0, tiled=True)
    size = units // CHUNKS
    hiddens, grad_pres, w_ins, w_outs = [], [], [], []
    slopes, h_scat, g_scat = [], [], []
    for c in range(CHUNKS):
        start = depth * units + c * size
        w_ins.append(lax.dynamic_slice_in_dim(w_in, start, size, 1))
        w_outs.append(lax.dynamic_slice_in_dim(w_out, start, size, 0))
    for c in range(CHUNKS):
        preact = lax.psum_scatter(
            jnp.dot(x_all, w_ins[c], preferred_element_type=jnp.float32).astype(jnp.bfloat16),
            "row", scatter_dimension=0, tiled=True,
        ).astype(jnp.float32)
        grad_hidden = lax.psum_scatter(
            lax.dot_general(
                dy_all, w_outs[c], (((1,), (1,)), ((), ())), preferred_element_type=jnp.float32
            ).astype(jnp.bfloat16),
            "row", scatter_dimension=0, tiled=True,
        )
        gelu_value, gelu_slope = gelu_pair(preact)
        hiddens.append(lax.all_gather(gelu_value.astype(jnp.bfloat16), "row", axis=0, tiled=True))
        grad_pre = (grad_hidden.astype(jnp.float32) * gelu_slope).astype(jnp.bfloat16)
        grad_pres.append(lax.all_gather(grad_pre, "row", axis=0, tiled=True))
    outputs = 0.0
    grad_inputs = 0.0
    g_w_in, g_w_out = [], []
    half = w_out.shape[1] // n_depth
    for c in range(CHUNKS):
        g_w_out.append(lax.dot_general(
            hiddens[c], dy_all, (((0,), (0,)), ((), ())), preferred_element_type=jnp.float32
        ).astype(jnp.bfloat16))
        outputs += jnp.dot(hiddens[c], w_outs[c], preferred_element_type=jnp.float32)
        grad_inputs += lax.dot_general(
            grad_pres[c], w_ins[c], (((1,), (1,)), ((), ())), preferred_element_type=jnp.float32
        )
        g_w_in.append(lax.dot_general(
            x_all, grad_pres[c], (((0,), (0,)), ((), ())), preferred_element_type=jnp.float32
        ).astype(jnp.bfloat16))
    outputs = lax.psum_scatter(
        outputs.astype(jnp.bfloat16), ("depth", "col"), scatter_dimension=0, tiled=True)
    grad_inputs = lax.psum_scatter(
        grad_inputs.astype(jnp.bfloat16), ("depth", "col"), scatter_dimension=0, tiled=True)
    grad_w_in = jnp.concatenate(g_w_in, axis=1)
    grad_w_out = lax.all_to_all(
        jnp.concatenate(g_w_out, axis=0), "depth", split_axis=1, concat_axis=0, tiled=True)
    return (outputs, grad_inputs, grad_w_in, grad_w_out)


def solution(mesh):
    in_specs = (
        P(("depth", "col"), "row"),
        P(("depth", "col"), "row"),
        P("row", "col"),
        P("col", "row"),
    )
    out_specs = (
        P(("depth", "col"), "row"),
        P(("depth", "col"), "row"),
        P("row", ("col", "depth")),
        P("col", ("row", "depth")),
    )

    def body(*args):
        return on_device(mesh.shape["depth"], *args)

    return jax.shard_map(
        body, mesh=mesh, in_specs=in_specs, out_specs=out_specs, check_vma=False
    )
```

```python
import functools

import jax
import jax.numpy as jnp
from jax import lax
from jax.experimental import pallas as pl
from jax.experimental.pallas import tpu as pltpu
from jax.sharding import PartitionSpec as P

MESH = pl.DeviceIdType.MESH
BF16 = jnp.bfloat16
F32 = jnp.float32
UNITS = 256
TILE = 64

gelu_c = 0.7978845608028654
gelu_k = 0.044715


def gelu_pair(preact):
    inner = gelu_c * (preact + gelu_k * preact * preact * preact)
    tangent = jnp.tanh(inner)
    gelu_value = 0.5 * preact * (1.0 + tangent)
    gelu_slope = 0.5 * (1.0 + tangent) + 0.5 * preact * (1.0 - tangent * tangent) * gelu_c * (
        1.0 + 3.0 * gelu_k * preact * preact
    )
    return (gelu_value, gelu_slope)


def dot(a, b, ca, cb):
    return lax.dot_general(a, b, (((ca,), (cb,)), ((), ())), preferred_element_type=F32)


def kernel(
    n_row,
    x_ref, xt_ref, dy_ref, dyk_ref, dys_ref, w_in_hbm, w_out_hbm,
    sums_ref, gwi_hbm, gwo_hbm,
    w_in, w_out, acc_o, acc_g, pk, ps, pr, total, from_left, from_right, to_right, to_left,
    hg, gwi_st, gk_st, gs_st,
    w_sem, p_send, p_recv, p_free, r_send, r_recv, r_free, l_send, l_recv, l_free,
    h_send, h_recv, h_free, gwi_sem, gk_sem, gs_send, gs_recv,
):
    n_chunks, width, units = w_in.shape
    tokens = x_ref.shape[0]
    half = tokens // 2
    nz = n_row // 2
    slots = from_left.shape[0]
    row = lax.axis_index("row")
    depth = lax.axis_index("depth")
    z = row // 2
    core = row % 2
    mine = pl.multiple_of(core * half, half)
    other = pl.multiple_of((1 - core) * half, half)
    sibling = {"row": row + 1 - 2 * core}
    right = {"row": (row + 2) % n_row}
    left = {"row": (row + n_row - 2) % n_row}
    peer = {"depth": 1 - depth}
    first = depth * (n_chunks * units)

    def w_copy(c, q):
        at = pl.ds(pl.multiple_of(first + c * units, units), units)
        if q == 0:
            return pltpu.make_async_copy(w_in_hbm.at[:, at], w_in.at[c], w_sem.at[c, q])
        return pltpu.make_async_copy(w_out_hbm.at[at, :], w_out.at[c], w_sem.at[c, q])

    def remote(src, dst, send_sem, recv_sem, device):
        return pltpu.make_async_remote_copy(
            src_ref=src, dst_ref=dst, send_sem=send_sem, recv_sem=recv_sem,
            device_id=device, device_id_type=MESH,
        )

    def p_copy(c, q):
        s = c % 2
        return remote(ps.at[s, q], pr.at[s, q], p_send.at[s, q], p_recv.at[s, q], sibling)

    def r_copy(c, q):
        s, d = c % 2, c % slots
        return remote(to_right.at[s, q], from_left.at[d, q], r_send.at[s, q], r_recv.at[d, q], right)

    def l_copy(c, q):
        s, d = c % 2, c % slots
        return remote(to_left.at[s, q], from_right.at[d, q], l_send.at[s, q], l_recv.at[d, q], left)

    def h_copy(c, q):
        s = c % 2
        part = hg.at[s, q, pl.ds(mine, half), :]
        return remote(part, part, h_send.at[s, q], h_recv.at[s, q], sibling)

    def gwi_copy(c):
        at = pl.ds(pl.multiple_of(c * units, units), units)
        return pltpu.make_async_copy(gwi_st.at[c % 2], gwi_hbm.at[:, at], gwi_sem.at[c % 2])

    def gwo_rows(c):
        return gwo_hbm.at[pl.ds(pl.multiple_of(first + c * units, units), units), :]

    def gk_copy(c):
        return pltpu.make_async_copy(gk_st.at[c % 2], gwo_rows(c), gk_sem.at[c % 2])

    def gs_copy(c):
        return remote(gs_st.at[c % 2], gwo_rows(c), gs_send.at[c % 2], gs_recv.at[c], peer)

    def signal(sem, device):
        pl.semaphore_signal(sem, inc=1, device_id=device, device_id_type=MESH)

    @pl.loop(0, n_chunks)
    def _(c):
        w_copy(c, 0).start()
        w_copy(c, 1).start()

    barrier = pltpu.get_barrier_semaphore()
    signal(barrier, sibling)
    signal(barrier, peer)

    @pl.when(z > 0)
    def _():
        signal(barrier, left)

    @pl.when(z < nz - 1)
    def _():
        signal(barrier, right)

    acc_o[...] = jnp.zeros_like(acc_o)
    acc_g[...] = jnp.zeros_like(acc_g)

    @pl.when(z == 0)
    def _():
        from_left[...] = jnp.zeros_like(from_left)

    @pl.when(z == nz - 1)
    def _():
        from_right[...] = jnp.zeros_like(from_right)

    inner = jnp.logical_and(z > 0, z < nz - 1)
    pl.semaphore_wait(barrier, jnp.where(inner, 4, 3))

    def product(c, q):
        s = c % 2
        w_copy(c, q).wait()

        def part(start):
            if q == 0:
                value = dot(x_ref[pl.ds(start, half), :], w_in[c], 1, 0)
            else:
                value = dot(dy_ref[pl.ds(start, half), :], w_out[c], 1, 1)
            return value.astype(BF16)

        ps[s, q] = part(other)

        @pl.when(c >= 2)
        def _():
            pl.semaphore_wait(p_free.at[q], 1)

        p_copy(c, q).start()
        pk[s, q] = part(mine)

    def chip_sum(c, q):
        s, t = c % 2, c % nz
        p_copy(c, q).wait()

        @pl.loop(0, half, step=TILE)
        def _(i):
            at = pl.ds(pl.multiple_of(i, TILE), TILE)
            total[t, q, at, :] = pk[s, q, at, :].astype(F32) + pr[s, q, at, :].astype(F32)

        @pl.when(c < n_chunks - 2)
        def _():
            signal(p_free.at[q], sibling)

    def flow(c, q, copy, held, staged, free, has_before, has_after):
        s, t, d = c % 2, c % nz, c % slots

        @pl.when(has_before)
        def _():
            copy(c, q).wait_recv()

        @pl.when(has_after)
        def _():
            @pl.when(c >= 2)
            def _():
                copy(c, q).wait_send()

            @pl.loop(0, half, step=TILE)
            def _(i):
                at = pl.ds(pl.multiple_of(i, TILE), TILE)
                staged[s, q, at, :] = (
                    total[t, q, at, :] + held[d, q, at, :].astype(F32)
                ).astype(BF16)

            @pl.when(c >= slots)
            def _():
                pl.semaphore_wait(free.at[q], 1)

            copy(c, q).start()

    def activate(c):
        s, t, d = c % 2, c % nz, c % slots

        @pl.loop(0, half, step=TILE)
        def _(i):
            at = pl.ds(pl.multiple_of(i, TILE), TILE)
            preact, grad = (
                total[t, q, at, :]
                + from_left[d, q, at, :].astype(F32)
                + from_right[d, q, at, :].astype(F32)
                for q in range(2)
            )
            value, slope = gelu_pair(preact)
            to = pl.ds(pl.multiple_of(mine + i, TILE), TILE)
            hg[s, 0, to, :] = value.astype(BF16)
            hg[s, 1, to, :] = (grad.astype(BF16).astype(F32) * slope).astype(BF16)

        for q in range(2):

            @pl.when(jnp.logical_and(z > 0, c < n_chunks - slots))
            def _():
                signal(r_free.at[q], left)

            @pl.when(jnp.logical_and(z < nz - 1, c < n_chunks - slots))
            def _():
                signal(l_free.at[q], right)

            @pl.when(c >= 2)
            def _():
                pl.semaphore_wait(h_free.at[q], 1)

            h_copy(c, q).start()

    def rows_loop(body):
        step = min(256, tokens)

        @pl.loop(0, tokens, step=step)
        def _(i):
            body(pl.ds(pl.multiple_of(i, step), step))

    def finish(c, q):
        s = c % 2
        h_copy(c, q).wait()

        if q == 0:

            def add(at):
                acc_o[at, :] += dot(hg[s, 0, at, :], w_out[c], 1, 0)

            rows_loop(add)

            @pl.when(c >= 2)
            def _():
                gk_copy(c).wait()
                gs_copy(c).wait_send()

            gs_st[s] = dot(hg[s, 0], dys_ref[...], 0, 0).astype(BF16)
            gs_copy(c).start()
            gk_st[s] = dot(hg[s, 0], dyk_ref[...], 0, 0).astype(BF16)
            gk_copy(c).start()
        else:

            def add(at):
                acc_g[at, :] += dot(hg[s, 1, at, :], w_in[c], 1, 1)

            rows_loop(add)

            @pl.when(c >= 2)
            def _():
                gwi_copy(c).wait()

            gwi_st[s] = dot(xt_ref[...], hg[s, 1], 1, 0).astype(BF16)
            gwi_copy(c).start()

        @pl.when(c < n_chunks - 2)
        def _():
            signal(h_free.at[q], sibling)

    def at_chunk(c, body):
        @pl.when(jnp.logical_and(c >= 0, c < n_chunks))
        def _():
            body(c)

    @pl.loop(0, n_chunks + nz + 1)
    def _(step):
        for q in range(2):
            at_chunk(step - 1, lambda c: chip_sum(c, q))
            at_chunk(
                step - 1 - z,
                lambda c: flow(c, q, r_copy, from_left, to_right, r_free, z > 0, z < nz - 1),
            )
            at_chunk(
                step - nz + z,
                lambda c: flow(c, q, l_copy, from_right, to_left, l_free, z < nz - 1, z > 0),
            )
            at_chunk(step, lambda c: product(c, q))
            if q == 0:
                at_chunk(step - nz - 1, lambda c: finish(c, 0))
            else:
                at_chunk(step - nz, activate)
                at_chunk(step - nz - 1, lambda c: finish(c, 1))

    sums_ref[0] = acc_o[...].astype(BF16)
    sums_ref[1] = acc_g[...].astype(BF16)

    for c in (n_chunks - 2, n_chunks - 1):
        gwi_copy(c).wait()
        gk_copy(c).wait()
        gs_copy(c).wait_send()
        for q in range(2):

            @pl.when(z < nz - 1)
            def _():
                r_copy(c, q).wait_send()

            @pl.when(z > 0)
            def _():
                l_copy(c, q).wait_send()

    @pl.loop(0, n_chunks)
    def _(c):
        gs_copy(c).wait_recv()


def on_device(n_row, n_depth, inputs, cotangent, w_in, w_out):
    depth = lax.axis_index("depth")
    width = w_in.shape[0]
    units = w_in.shape[1] // n_depth
    both = lax.all_gather(
        jnp.stack([inputs, cotangent]), ("depth", "col"), axis=1, tiled=True
    )
    x_all, dy_all = both[0], both[1]
    tokens = x_all.shape[0]
    part = width // n_depth
    dy_keep = lax.dynamic_slice_in_dim(dy_all, depth * part, part, 1)
    dy_send = lax.dynamic_slice_in_dim(dy_all, (1 - depth) * part, part, 1)
    n_chunks = units // UNITS
    half = tokens // 2
    nz = n_row // 2
    slots = nz + 1
    dma, regular = pltpu.SemaphoreType.DMA, pltpu.SemaphoreType.REGULAR
    vmem, hbm = pl.BlockSpec(memory_space=pltpu.VMEM), pl.BlockSpec(memory_space=pl.ANY)
    sums, grad_w_in, grad_w_out = pl.pallas_call(
        functools.partial(kernel, n_row),
        out_shape=(
            jax.ShapeDtypeStruct((2, tokens, width), BF16),
            jax.ShapeDtypeStruct((width, units), BF16),
            jax.ShapeDtypeStruct((w_out.shape[0], part), BF16),
        ),
        in_specs=[vmem] * 5 + [hbm] * 2,
        out_specs=(vmem, hbm, hbm),
        scratch_shapes=[
            pltpu.VMEM((n_chunks, width, UNITS), BF16),
            pltpu.VMEM((n_chunks, UNITS, width), BF16),
            pltpu.VMEM((tokens, width), F32),
            pltpu.VMEM((tokens, width), F32),
            pltpu.VMEM((2, 2, half, UNITS), BF16),
            pltpu.VMEM((2, 2, half, UNITS), BF16),
            pltpu.VMEM((2, 2, half, UNITS), BF16),
            pltpu.VMEM((nz, 2, half, UNITS), F32),
            pltpu.VMEM((slots, 2, half, UNITS), BF16),
            pltpu.VMEM((slots, 2, half, UNITS), BF16),
            pltpu.VMEM((2, 2, half, UNITS), BF16),
            pltpu.VMEM((2, 2, half, UNITS), BF16),
            pltpu.VMEM((2, 2, tokens, UNITS), BF16),
            pltpu.VMEM((2, width, UNITS), BF16),
            pltpu.VMEM((2, UNITS, part), BF16),
            pltpu.VMEM((2, UNITS, part), BF16),
            dma((n_chunks, 2)),
            dma((2, 2)), dma((2, 2)), regular((2,)),
            dma((2, 2)), dma((slots, 2)), regular((2,)),
            dma((2, 2)), dma((slots, 2)), regular((2,)),
            dma((2, 2)), dma((2, 2)), regular((2,)),
            dma((2,)), dma((2,)), dma((2,)), dma((n_chunks,)),
        ],
        compiler_params=pltpu.CompilerParams(
            collective_id=0, has_side_effects=True, vmem_limit_bytes=60 * 1024 * 1024
        ),
        cost_estimate=pl.CostEstimate(
            flops=12 * tokens * width * units, bytes_accessed=6 * width * units * 2,
            transcendentals=tokens * units,
        ),
    )(x_all, x_all.T, dy_all, dy_keep, dy_send, w_in, w_out)
    sums = lax.psum_scatter(sums, ("depth", "col"), scatter_dimension=1, tiled=True)
    return (sums[0], sums[1], grad_w_in, grad_w_out)


def solution(mesh):
    in_specs = (
        P(("depth", "col"), "row"),
        P(("depth", "col"), "row"),
        P("row", "col"),
        P("col", "row"),
    )
    out_specs = (
        P(("depth", "col"), "row"),
        P(("depth", "col"), "row"),
        P("row", ("col", "depth")),
        P("col", ("row", "depth")),
    )
    return jax.shard_map(
        functools.partial(on_device, mesh.shape["row"], mesh.shape["depth"]),
        mesh=mesh, in_specs=in_specs, out_specs=out_specs, check_vma=False,
    )
```

```python
import functools

import jax
import jax.numpy as jnp
from jax import lax
from jax.experimental import pallas as pl
from jax.experimental.pallas import tpu as pltpu
from jax.sharding import PartitionSpec as P

MESH = pl.DeviceIdType.MESH
BF16 = jnp.bfloat16
F32 = jnp.float32
UNITS = 256
TILE = 64

gelu_c = 0.7978845608028654
gelu_k = 0.044715


def gelu_pair(preact):
    inner = gelu_c * (preact + gelu_k * preact * preact * preact)
    tangent = jnp.tanh(inner)
    gelu_value = 0.5 * preact * (1.0 + tangent)
    gelu_slope = 0.5 * (1.0 + tangent) + 0.5 * preact * (1.0 - tangent * tangent) * gelu_c * (
        1.0 + 3.0 * gelu_k * preact * preact
    )
    return (gelu_value, gelu_slope)


def dot(a, b, ca, cb):
    return lax.dot_general(a, b, (((ca,), (cb,)), ((), ())), preferred_element_type=F32)


def kernel(
    n_row, n_depth, n_col,
    x_block, dy_block, w_in_hbm, w_out_hbm,
    out_ref, gin_ref, gwi_hbm, gwo_hbm,
    x_ref, xt_ref, dy_ref, dyk_ref, dys_ref, sums, parts,
    w_in, w_out, acc_o, acc_g, pk, ps, pr, total, from_left, from_right, to_right, to_left,
    hg, gwi_st, gk_st, gs_st,
    w_sem, p_send, p_recv, p_free, r_send, r_recv, r_free, l_send, l_recv, l_free,
    h_send, h_recv, h_free, gwi_sem, gk_sem, gs_send, gs_recv,
    a_send, a_recv, s_send, s_recv,
):
    n_chunks, width, units = w_in.shape
    n_sub = 2 * n_chunks
    tokens = x_ref.shape[0]
    half = tokens // 2
    quarter = half // 2
    block = x_block.shape[0]
    n_plane = n_depth * n_col
    nz = n_row // 2
    slots = from_left.shape[0]
    stages = to_right.shape[0]
    row = lax.axis_index("row")
    depth = lax.axis_index("depth")
    plane = depth * n_col + lax.axis_index("col")
    z = row // 2
    core = row % 2
    sibling = {"row": row + 1 - 2 * core}
    right = {"row": (row + 2) % n_row}
    left = {"row": (row + n_row - 2) % n_row}
    peer = {"depth": 1 - depth}
    first = depth * (n_chunks * units)

    def rows_of(u, which):
        return pl.ds(pl.multiple_of((u % 2) * half + which * quarter, quarter), quarter)

    def plane_peer(k):
        other = (plane + k) % n_plane
        return other, {"depth": other // n_col, "col": other % n_col}

    def block_rows(index):
        return pl.ds(pl.multiple_of(index * block, block), block)

    def a_copy(q, k):
        src, dst = ((x_block, x_ref), (dy_block, dy_ref))[q]
        return remote(
            src, dst.at[block_rows(plane), :], a_send.at[q, k - 1], a_recv.at[q, k - 1],
            plane_peer(k)[1],
        )

    def s_copy(q, k):
        other, device = plane_peer(k)
        return remote(
            sums.at[q, block_rows(other), :], parts.at[q, k - 1],
            s_send.at[q, k - 1], s_recv.at[q, k - 1], device,
        )

    def w_copy(c, q):
        at = pl.ds(pl.multiple_of(first + c * units, units), units)
        if q == 0:
            return pltpu.make_async_copy(w_in_hbm.at[:, at], w_in.at[c], w_sem.at[c, q])
        return pltpu.make_async_copy(w_out_hbm.at[at, :], w_out.at[c], w_sem.at[c, q])

    def remote(src, dst, send_sem, recv_sem, device):
        return pltpu.make_async_remote_copy(
            src_ref=src, dst_ref=dst, send_sem=send_sem, recv_sem=recv_sem,
            device_id=device, device_id_type=MESH,
        )

    def p_copy(c, q):
        s = c % 2
        return remote(ps.at[s, q], pr.at[s, q], p_send.at[s, q], p_recv.at[s, q], sibling)

    def r_copy(c, q):
        s, d = c % stages, c % slots
        return remote(to_right.at[s, q], from_left.at[d, q], r_send.at[s, q], r_recv.at[d, q], right)

    def l_copy(c, q):
        s, d = c % stages, c % slots
        return remote(to_left.at[s, q], from_right.at[d, q], l_send.at[s, q], l_recv.at[d, q], left)

    def h_copy(u, q):
        s, t = (u // 2) % 2, u % 2
        part = hg.at[s, q, rows_of(u, core), :]
        return remote(part, part, h_send.at[s, t, q], h_recv.at[s, t, q], sibling)

    def gwi_copy(c):
        at = pl.ds(pl.multiple_of(c * units, units), units)
        return pltpu.make_async_copy(gwi_st.at[c % 2], gwi_hbm.at[:, at], gwi_sem.at[c % 2])

    def gwo_rows(c):
        return gwo_hbm.at[pl.ds(pl.multiple_of(first + c * units, units), units), :]

    def gk_copy(c):
        return pltpu.make_async_copy(gk_st.at[c % 2], gwo_rows(c), gk_sem.at[c % 2])

    def gs_copy(c):
        return remote(gs_st.at[c % 2], gwo_rows(c), gs_send.at[c % 2], gs_recv.at[c], peer)

    def signal(sem, device):
        pl.semaphore_signal(sem, inc=1, device_id=device, device_id_type=MESH)

    @pl.loop(0, n_chunks)
    def _(c):
        w_copy(c, 0).start()
        w_copy(c, 1).start()

    barrier = pltpu.get_barrier_semaphore()
    signal(barrier, sibling)
    for k in range(1, n_plane):
        signal(barrier, plane_peer(k)[1])

    @pl.when(z > 0)
    def _():
        signal(barrier, left)

    @pl.when(z < nz - 1)
    def _():
        signal(barrier, right)

    acc_o[...] = jnp.zeros_like(acc_o)
    acc_g[...] = jnp.zeros_like(acc_g)

    @pl.when(z == 0)
    def _():
        from_left[...] = jnp.zeros_like(from_left)

    @pl.when(z == nz - 1)
    def _():
        from_right[...] = jnp.zeros_like(from_right)

    inner = jnp.logical_and(z > 0, z < nz - 1)
    pl.semaphore_wait(barrier, jnp.where(inner, n_plane + 2, n_plane + 1))

    for q in range(2):
        for k in range(1, n_plane):
            a_copy(q, k).start()
    x_ref[block_rows(plane), :] = x_block[...]
    dy_ref[block_rows(plane), :] = dy_block[...]

    def gathered(q):
        for k in range(1, n_plane):
            a_copy(q, k).wait()

    def arrange():
        part = width // 2
        for d in range(2):

            @pl.when(depth == d)
            def _():
                dyk_ref[...] = dy_ref[:, d * part:(d + 1) * part]
                dys_ref[...] = dy_ref[:, (1 - d) * part:(2 - d) * part]

        for i in range(0, tokens, half // 2):
            xt_ref[:, i:i + half // 2] = x_ref[i:i + half // 2, :].T

    def product(u, q):
        s, c = u % 2, u // 2

        @pl.when(u == 0)
        def _():
            gathered(q)

        @pl.when(u % 2 == 0)
        def _():
            w_copy(c, q).wait()

        def part(which):
            if q == 0:
                value = dot(x_ref[rows_of(u, which), :], w_in[c], 1, 0)
            else:
                value = dot(dy_ref[rows_of(u, which), :], w_out[c], 1, 1)
            return value.astype(BF16)

        ps[s, q] = part(1 - core)

        @pl.when(u >= 2)
        def _():
            pl.semaphore_wait(p_free.at[q], 1)

        p_copy(u, q).start()
        pk[s, q] = part(core)

    def chip_sum(c, q):
        s, t = c % 2, c % nz
        p_copy(c, q).wait()

        @pl.loop(0, quarter, step=TILE)
        def _(i):
            at = pl.ds(pl.multiple_of(i, TILE), TILE)
            total[t, q, at, :] = pk[s, q, at, :].astype(F32) + pr[s, q, at, :].astype(F32)

        @pl.when(c < n_sub - 2)
        def _():
            signal(p_free.at[q], sibling)

    def flow(c, q, copy, held, staged, free, has_before, has_after):
        s, t, d = c % stages, c % nz, c % slots

        @pl.when(has_before)
        def _():
            copy(c, q).wait_recv()

        @pl.when(has_after)
        def _():
            @pl.when(c >= stages)
            def _():
                copy(c, q).wait_send()

            @pl.loop(0, quarter, step=TILE)
            def _(i):
                at = pl.ds(pl.multiple_of(i, TILE), TILE)
                staged[s, q, at, :] = (
                    total[t, q, at, :] + held[d, q, at, :].astype(F32)
                ).astype(BF16)

            @pl.when(c >= slots)
            def _():
                pl.semaphore_wait(free.at[q], 1)

            copy(c, q).start()

    def activate(c):
        s, t, d = (c // 2) % 2, c % nz, c % slots
        mine = (c % 2) * half + core * quarter

        @pl.loop(0, quarter, step=TILE)
        def _(i):
            at = pl.ds(pl.multiple_of(i, TILE), TILE)
            preact, grad = (
                total[t, q, at, :]
                + from_left[d, q, at, :].astype(F32)
                + from_right[d, q, at, :].astype(F32)
                for q in range(2)
            )
            value, slope = gelu_pair(preact)
            to = pl.ds(pl.multiple_of(mine + i, TILE), TILE)
            hg[s, 0, to, :] = value.astype(BF16)
            hg[s, 1, to, :] = (grad.astype(BF16).astype(F32) * slope).astype(BF16)

        for q in range(2):

            @pl.when(jnp.logical_and(z > 0, c < n_sub - slots))
            def _():
                signal(r_free.at[q], left)

            @pl.when(jnp.logical_and(z < nz - 1, c < n_sub - slots))
            def _():
                signal(l_free.at[q], right)

            @pl.when(jnp.logical_and(c >= 4, c % 2 == 0))
            def _():
                pl.semaphore_wait(h_free.at[q], 1)

            h_copy(c, q).start()

    def rows_loop(body):
        step = min(256, tokens)

        @pl.loop(0, tokens, step=step)
        def _(i):
            body(pl.ds(pl.multiple_of(i, step), step))

    def finish(c, q):
        s = c % 2
        h_copy(2 * c, q).wait()
        h_copy(2 * c + 1, q).wait()

        if q == 0:

            def add(at):
                acc_o[at, :] += dot(hg[s, 0, at, :], w_out[c], 1, 0)

            rows_loop(add)

            @pl.when(c >= 2)
            def _():
                gk_copy(c).wait()
                gs_copy(c).wait_send()

            gs_st[s] = dot(hg[s, 0], dys_ref[...], 0, 0).astype(BF16)
            gs_copy(c).start()
            gk_st[s] = dot(hg[s, 0], dyk_ref[...], 0, 0).astype(BF16)
            gk_copy(c).start()
        else:

            def add(at):
                acc_g[at, :] += dot(hg[s, 1, at, :], w_in[c], 1, 1)

            rows_loop(add)

            @pl.when(c >= 2)
            def _():
                gwi_copy(c).wait()

            gwi_st[s] = dot(xt_ref[...], hg[s, 1], 1, 0).astype(BF16)
            gwi_copy(c).start()

        @pl.when(c < n_chunks - 2)
        def _():
            signal(h_free.at[q], sibling)

    def at_sub(u, body):
        @pl.when(jnp.logical_and(u >= 0, u < n_sub))
        def _():
            body(u)

    @pl.loop(0, n_sub + nz + 2)
    def _(step):
        for q in range(2):
            at_sub(step - 1, lambda u: chip_sum(u, q))
            at_sub(
                step - 1 - z,
                lambda u: flow(u, q, r_copy, from_left, to_right, r_free, z > 0, z < nz - 1),
            )
            at_sub(
                step - nz + z,
                lambda u: flow(u, q, l_copy, from_right, to_left, l_free, z < nz - 1, z > 0),
            )
            at_sub(step, lambda u: product(u, q))
            if q == 1:
                at_sub(step - nz, activate)

        @pl.when(step == 1)
        def _():
            arrange()

        def last_products(u):
            for q in range(2):

                @pl.when(u % 2 == q)
                def _():
                    finish(u // 2, q)

        at_sub(step - nz - 2, last_products)

    for q, acc in enumerate((acc_o, acc_g)):
        sums[q] = acc[...].astype(BF16)
        for k in range(1, n_plane):
            s_copy(q, k).start()

    for c in (n_chunks - 2, n_chunks - 1):
        gwi_copy(c).wait()
        gk_copy(c).wait()
        gs_copy(c).wait_send()

    for u in range(n_sub - stages, n_sub):
        for q in range(2):

            @pl.when(z < nz - 1)
            def _():
                r_copy(u, q).wait_send()

            @pl.when(z > 0)
            def _():
                l_copy(u, q).wait_send()

    for q, ref in enumerate((out_ref, gin_ref)):
        for k in range(1, n_plane):
            s_copy(q, k).wait()
        value = sums[q, block_rows(plane), :].astype(F32)
        for k in range(1, n_plane):
            value += parts[q, k - 1].astype(F32)
        ref[...] = value.astype(BF16)

    @pl.loop(0, n_chunks)
    def _(c):
        gs_copy(c).wait_recv()


def copy_kernel(a_ref, b_ref, a_out, b_out):
    a_out[...] = a_ref[...]
    b_out[...] = b_ref[...]


def copied(a, b, steps=8):
    specs = [pl.BlockSpec((v.shape[0] // steps, v.shape[1]), lambda i: (i, 0)) for v in (a, b)]
    return pl.pallas_call(
        copy_kernel, grid=(steps,), in_specs=specs, out_specs=specs,
        out_shape=[jax.ShapeDtypeStruct(v.shape, v.dtype) for v in (a, b)],
        compiler_params=pltpu.CompilerParams(vmem_limit_bytes=60 * 1024 * 1024),
    )(a, b)


def on_device(n_row, n_depth, n_col, inputs, cotangent, w_in, w_out):
    width = w_in.shape[0]
    units = w_in.shape[1] // n_depth
    block = inputs.shape[0]
    n_plane = n_depth * n_col
    tokens = block * n_plane
    part = width // n_depth
    n_chunks = units // UNITS
    quarter = tokens // 4
    nz = n_row // 2
    slots, stages = nz + 3, 3
    dma, regular = pltpu.SemaphoreType.DMA, pltpu.SemaphoreType.REGULAR
    vmem, hbm = pl.BlockSpec(memory_space=pltpu.VMEM), pl.BlockSpec(memory_space=pl.ANY)
    outputs, grad_inputs, grad_w_in, grad_w_out = pl.pallas_call(
        functools.partial(kernel, n_row, n_depth, n_col),
        out_shape=(
            jax.ShapeDtypeStruct((block, width), BF16),
            jax.ShapeDtypeStruct((block, width), BF16),
            jax.ShapeDtypeStruct((width, units), BF16),
            jax.ShapeDtypeStruct((w_out.shape[0], part), BF16),
        ),
        in_specs=[vmem] * 2 + [hbm] * 2,
        out_specs=(vmem, vmem, hbm, hbm),
        scratch_shapes=[
            pltpu.VMEM((tokens, width), BF16),
            pltpu.VMEM((width, tokens), BF16),
            pltpu.VMEM((tokens, width), BF16),
            pltpu.VMEM((tokens, part), BF16),
            pltpu.VMEM((tokens, part), BF16),
            pltpu.VMEM((2, tokens, width), BF16),
            pltpu.VMEM((2, n_plane - 1, block, width), BF16),
            pltpu.VMEM((n_chunks, width, UNITS), BF16),
            pltpu.VMEM((n_chunks, UNITS, width), BF16),
            pltpu.VMEM((tokens, width), F32),
            pltpu.VMEM((tokens, width), F32),
            pltpu.VMEM((2, 2, quarter, UNITS), BF16),
            pltpu.VMEM((2, 2, quarter, UNITS), BF16),
            pltpu.VMEM((2, 2, quarter, UNITS), BF16),
            pltpu.VMEM((nz, 2, quarter, UNITS), F32),
            pltpu.VMEM((slots, 2, quarter, UNITS), BF16),
            pltpu.VMEM((slots, 2, quarter, UNITS), BF16),
            pltpu.VMEM((stages, 2, quarter, UNITS), BF16),
            pltpu.VMEM((stages, 2, quarter, UNITS), BF16),
            pltpu.VMEM((2, 2, tokens, UNITS), BF16),
            pltpu.VMEM((2, width, UNITS), BF16),
            pltpu.VMEM((2, UNITS, part), BF16),
            pltpu.VMEM((2, UNITS, part), BF16),
            dma((n_chunks, 2)),
            dma((2, 2)), dma((2, 2)), regular((2,)),
            dma((stages, 2)), dma((slots, 2)), regular((2,)),
            dma((stages, 2)), dma((slots, 2)), regular((2,)),
            dma((2, 2, 2)), dma((2, 2, 2)), regular((2,)),
            dma((2,)), dma((2,)), dma((2,)), dma((n_chunks,)),
            dma((2, n_plane - 1)), dma((2, n_plane - 1)), dma((2, n_plane - 1)), dma((2, n_plane - 1)),
        ],
        compiler_params=pltpu.CompilerParams(
            collective_id=0, has_side_effects=True, vmem_limit_bytes=60 * 1024 * 1024
        ),
        cost_estimate=pl.CostEstimate(
            flops=12 * tokens * width * units, bytes_accessed=6 * width * units * 2,
            transcendentals=tokens * units,
        ),
    )(inputs, cotangent, w_in, w_out)
    grad_w_in, grad_w_out = copied(grad_w_in, grad_w_out)
    return (outputs, grad_inputs, grad_w_in, grad_w_out)


def solution(mesh):
    in_specs = (
        P(("depth", "col"), "row"),
        P(("depth", "col"), "row"),
        P("row", "col"),
        P("col", "row"),
    )
    out_specs = (
        P(("depth", "col"), "row"),
        P(("depth", "col"), "row"),
        P("row", ("col", "depth")),
        P("col", ("row", "depth")),
    )
    return jax.shard_map(
        functools.partial(on_device, *(mesh.shape[a] for a in ("row", "depth", "col"))),
        mesh=mesh, in_specs=in_specs, out_specs=out_specs, check_vma=False,
    )
```

```python
import functools

import jax
import jax.numpy as jnp
from jax import lax
from jax.experimental import pallas as pl
from jax.experimental.pallas import tpu as pltpu
from jax.sharding import PartitionSpec as P

MESH = pl.DeviceIdType.MESH
BF16 = jnp.bfloat16
F32 = jnp.float32
UNITS = 256
TILE = 128

gelu_c = 0.7978845608028654
gelu_k = 0.044715


def gelu_pair(preact):
    inner = gelu_c * (preact + gelu_k * preact * preact * preact)
    tangent = jnp.tanh(inner)
    gelu_value = 0.5 * preact * (1.0 + tangent)
    gelu_slope = 0.5 * (1.0 + tangent) + 0.5 * preact * (1.0 - tangent * tangent) * gelu_c * (
        1.0 + 3.0 * gelu_k * preact * preact
    )
    return (gelu_value, gelu_slope)


def dot(a, b, ca, cb):
    return lax.dot_general(a, b, (((ca,), (cb,)), ((), ())), preferred_element_type=F32)


def kernel(
    n_row, n_depth, n_col,
    x_block, dy_block, w_in_hbm, w_out_hbm,
    out_ref, gin_ref, gwi_hbm, gwo_hbm,
    x_ref, xt_ref, dy_ref, dyo_ref, sums, parts,
    w_in, w_out, acc_o, acc_g, ps, pr, total, from_left, from_right, to_right, to_left,
    hg, gwi_st, gk_st, gs_st,
    w_sem, p_send, p_recv, p_free, r_send, r_recv, r_free, l_send, l_recv, l_free,
    h_send, h_recv, h_free, gwi_sem, gk_sem, gs_send, gs_recv,
    a_send, a_recv, s_send, s_recv,
):
    n_chunks, width, units = w_in.shape
    n_sub = 2 * n_chunks
    tokens = x_ref.shape[0]
    half = tokens // 2
    quarter = half // 2
    block = x_block.shape[0]
    n_plane = n_depth * n_col
    nz = n_row // 2
    slots = from_left.shape[0]
    stages = to_right.shape[0]
    row = lax.axis_index("row")
    depth = lax.axis_index("depth")
    col = lax.axis_index("col")
    plane = depth * n_col + col
    z = row // 2
    core = row % 2
    sibling = {"row": row + 1 - 2 * core}
    right = {"row": (row + 2) % n_row}
    left = {"row": (row + n_row - 2) % n_row}
    peer = {"depth": 1 - depth}
    first = depth * (n_chunks * units)

    def first_row(u):
        return ((u + depth) % 2) * half

    def rows_of(u, which):
        return pl.ds(pl.multiple_of(first_row(u) + which * quarter, quarter), quarter)

    def plane_peer(k):
        d, c = (depth + k // n_col) % n_depth, (col + k % n_col) % n_col
        return d * n_col + c, {"depth": d, "col": c}

    def block_rows(index):
        return pl.ds(pl.multiple_of(index * block, block), block)

    def a_copy(q, k):
        src, dst = ((x_block, x_ref), (dy_block, dy_ref))[q]
        return remote(
            src, dst.at[block_rows(plane), :], a_send.at[q, k - 1], a_recv.at[q, k - 1],
            plane_peer(k)[1],
        )

    def s_copy(q, k):
        other, device = plane_peer(k)
        return remote(
            sums.at[q, block_rows(other), :], parts.at[q, k - 1],
            s_send.at[q, k - 1], s_recv.at[q, k - 1], device,
        )

    def w_copy(c, q):
        at = pl.ds(pl.multiple_of(first + c * units, units), units)
        if q == 0:
            return pltpu.make_async_copy(w_in_hbm.at[:, at], w_in.at[c], w_sem.at[c, q])
        return pltpu.make_async_copy(w_out_hbm.at[at, :], w_out.at[c], w_sem.at[c, q])

    def remote(src, dst, send_sem, recv_sem, device):
        return pltpu.make_async_remote_copy(
            src_ref=src, dst_ref=dst, send_sem=send_sem, recv_sem=recv_sem,
            device_id=device, device_id_type=MESH,
        )

    def p_copy(c, q):
        s = c % 2
        return remote(ps.at[s, q, 1 - core], pr.at[s, q], p_send.at[s, q], p_recv.at[s, q], sibling)

    def r_copy(c, q):
        s, d = c % stages, c % slots
        return remote(to_right.at[s, q], from_left.at[d, q], r_send.at[s, q], r_recv.at[d, q], right)

    def l_copy(c, q):
        s, d = c % stages, c % slots
        return remote(to_left.at[s, q], from_right.at[d, q], l_send.at[s, q], l_recv.at[d, q], left)

    def h_copy(u, q):
        s, t = (u // 2) % 2, u % 2
        part = hg.at[s, q, rows_of(u, core), :]
        return remote(part, part, h_send.at[s, t, q], h_recv.at[s, t, q], sibling)

    def gwi_copy(c):
        at = pl.ds(pl.multiple_of(c * units, units), units)
        return pltpu.make_async_copy(gwi_st.at[c % 2], gwi_hbm.at[:, at], gwi_sem.at[c % 2])

    def gwo_rows(c):
        return gwo_hbm.at[pl.ds(pl.multiple_of(first + c * units, units), units), :]

    def gk_copy(c):
        return pltpu.make_async_copy(gk_st.at[c % 2], gwo_rows(c), gk_sem.at[c % 2])

    def gs_copy(c):
        return remote(gs_st.at[c % 2], gwo_rows(c), gs_send.at[c % 2], gs_recv.at[c], peer)

    def signal(sem, device):
        pl.semaphore_signal(sem, inc=1, device_id=device, device_id_type=MESH)

    @pl.loop(0, n_chunks)
    def _(c):
        w_copy(c, 0).start()
        w_copy(c, 1).start()

    barrier = pltpu.get_barrier_semaphore()
    signal(barrier, sibling)
    for k in range(1, n_plane):
        signal(barrier, plane_peer(k)[1])

    @pl.when(z > 0)
    def _():
        signal(barrier, left)

    @pl.when(z < nz - 1)
    def _():
        signal(barrier, right)

    acc_o[...] = jnp.zeros_like(acc_o)
    acc_g[...] = jnp.zeros_like(acc_g)

    @pl.when(z == 0)
    def _():
        from_left[...] = jnp.zeros_like(from_left)

    @pl.when(z == nz - 1)
    def _():
        from_right[...] = jnp.zeros_like(from_right)

    inner = jnp.logical_and(z > 0, z < nz - 1)
    pl.semaphore_wait(barrier, jnp.where(inner, n_plane + 2, n_plane + 1))

    for ks in (range(1, n_col + 1), range(n_col + 1, n_plane)):
        for q in range(2):
            for k in ks:
                a_copy(q, k).start()
    x_ref[block_rows(plane), :] = x_block[...]
    dy_ref[block_rows(plane), :] = dy_block[...]

    def gathered(q, t):
        for k in range(1, n_col) if t == 0 else range(n_col, n_plane):
            a_copy(q, k).wait()

    def arrange():
        part = width // 2
        for d in range(2):

            @pl.when(depth == d)
            def _():
                dyo_ref[:, :part] = dy_ref[:, d * part:(d + 1) * part]
                dyo_ref[:, part:] = dy_ref[:, (1 - d) * part:(2 - d) * part]

        for i in range(0, tokens, half // 2):
            xt_ref[:, i:i + half // 2] = x_ref[i:i + half // 2, :].T

    def product(u, q):
        s, c = u % 2, u // 2

        for t in range(2):

            @pl.when(u == t)
            def _():
                gathered(q, t)

        @pl.when(u % 2 == 0)
        def _():
            w_copy(c, q).wait()

        rows = pl.ds(pl.multiple_of(first_row(u), half), half)
        if q == 0:
            value = dot(x_ref[rows, :], w_in[c], 1, 0)
        else:
            value = dot(dy_ref[rows, :], w_out[c], 1, 1)
        ps[s, q] = value.astype(BF16).reshape(2, quarter, units)

        @pl.when(u >= 2)
        def _():
            pl.semaphore_wait(p_free.at[q], 1)

        p_copy(u, q).start()

    def chip_sum(c, q):
        s, t = c % 2, c % nz
        p_copy(c, q).wait()

        for i in range(0, quarter, TILE):
            at = pl.ds(i, TILE)
            total[t, q, at, :] = ps[s, q, core, at, :].astype(F32) + pr[s, q, at, :].astype(F32)

        @pl.when(c < n_sub - 2)
        def _():
            signal(p_free.at[q], sibling)

    def flow(c, q, copy, held, staged, free, has_before, has_after):
        s, t, d = c % stages, c % nz, c % slots

        @pl.when(has_before)
        def _():
            copy(c, q).wait_recv()

        @pl.when(has_after)
        def _():
            @pl.when(c >= stages)
            def _():
                copy(c, q).wait_send()

            for i in range(0, quarter, TILE):
                at = pl.ds(i, TILE)
                staged[s, q, at, :] = (
                    total[t, q, at, :] + held[d, q, at, :].astype(F32)
                ).astype(BF16)

            @pl.when(c >= slots)
            def _():
                pl.semaphore_wait(free.at[q], 1)

            copy(c, q).start()

    def activate(c):
        s, t, d = (c // 2) % 2, c % nz, c % slots
        mine = first_row(c) + core * quarter

        @pl.loop(0, quarter, step=TILE)
        def _(i):
            at = pl.ds(pl.multiple_of(i, TILE), TILE)
            preact, grad = (
                total[t, q, at, :]
                + from_left[d, q, at, :].astype(F32)
                + from_right[d, q, at, :].astype(F32)
                for q in range(2)
            )
            value, slope = gelu_pair(preact)
            to = pl.ds(pl.multiple_of(mine + i, TILE), TILE)
            hg[s, 0, to, :] = value.astype(BF16)
            hg[s, 1, to, :] = (grad.astype(BF16).astype(F32) * slope).astype(BF16)

        for q in range(2):

            @pl.when(jnp.logical_and(z > 0, c < n_sub - slots))
            def _():
                signal(r_free.at[q], left)

            @pl.when(jnp.logical_and(z < nz - 1, c < n_sub - slots))
            def _():
                signal(l_free.at[q], right)

            @pl.when(jnp.logical_and(c >= 4, c % 2 == 0))
            def _():
                pl.semaphore_wait(h_free.at[q], 1)

            h_copy(c, q).start()

    def rows_loop(body):
        step = min(512, tokens)

        @pl.loop(0, tokens, step=step)
        def _(i):
            body(pl.ds(pl.multiple_of(i, step), step))

    def finish(c, q):
        s = c % 2
        h_copy(2 * c, q).wait()
        h_copy(2 * c + 1, q).wait()

        if q == 0:

            def add(at):
                acc_o[at, :] += dot(hg[s, 0, at, :], w_out[c], 1, 0)

            rows_loop(add)

            @pl.when(c >= 2)
            def _():
                gk_copy(c).wait()
                gs_copy(c).wait_send()

            value = dot(hg[s, 0], dyo_ref[...], 0, 0).astype(BF16)
            gs_st[s] = value[:, width // 2:]
            gs_copy(c).start()
            gk_st[s] = value[:, :width // 2]
            gk_copy(c).start()
        else:

            def add(at):
                acc_g[at, :] += dot(hg[s, 1, at, :], w_in[c], 1, 1)

            rows_loop(add)

            @pl.when(c >= 2)
            def _():
                gwi_copy(c).wait()

            gwi_st[s] = dot(xt_ref[...], hg[s, 1], 1, 0).astype(BF16)
            gwi_copy(c).start()

        @pl.when(c < n_chunks - 2)
        def _():
            signal(h_free.at[q], sibling)

    def at_sub(u, body):
        @pl.when(jnp.logical_and(u >= 0, u < n_sub))
        def _():
            body(u)

    @pl.loop(0, n_sub + nz + 2)
    def _(step):
        for q in range(2):
            at_sub(step - 1, lambda u: chip_sum(u, q))
            at_sub(
                step - 1 - z,
                lambda u: flow(u, q, r_copy, from_left, to_right, r_free, z > 0, z < nz - 1),
            )
            at_sub(
                step - nz + z,
                lambda u: flow(u, q, l_copy, from_right, to_left, l_free, z < nz - 1, z > 0),
            )
            at_sub(step, lambda u: product(u, q))
            if q == 1:
                at_sub(step - nz, activate)

        @pl.when(step == 2)
        def _():
            arrange()

        def last_products(u):
            for q in range(2):

                @pl.when(u % 2 == q)
                def _():
                    finish(u // 2, q)

                @pl.when(u == n_sub - 2 + q)
                def _():
                    sums[q] = (acc_o, acc_g)[q][...].astype(BF16)
                    for k in range(1, n_plane):
                        s_copy(q, k).start()

        at_sub(step - nz - 2, last_products)

    for c in (n_chunks - 2, n_chunks - 1):
        gwi_copy(c).wait()
        gk_copy(c).wait()
        gs_copy(c).wait_send()

    for u in range(n_sub - stages, n_sub):
        for q in range(2):

            @pl.when(z < nz - 1)
            def _():
                r_copy(u, q).wait_send()

            @pl.when(z > 0)
            def _():
                l_copy(u, q).wait_send()

    for q, ref in enumerate((out_ref, gin_ref)):
        for k in range(1, n_plane):
            s_copy(q, k).wait()
        value = sums[q, block_rows(plane), :].astype(F32)
        for k in range(1, n_plane):
            value += parts[q, k - 1].astype(F32)
        ref[...] = value.astype(BF16)

    @pl.loop(0, n_chunks)
    def _(c):
        gs_copy(c).wait_recv()


def copy_kernel(a_ref, b_ref, a_out, b_out):
    a_out[...] = a_ref[...]
    b_out[...] = b_ref[...]


def copied(a, b, steps=8):
    specs = [pl.BlockSpec((v.shape[0] // steps, v.shape[1]), lambda i: (i, 0)) for v in (a, b)]
    return pl.pallas_call(
        copy_kernel, grid=(steps,), in_specs=specs, out_specs=specs,
        out_shape=[jax.ShapeDtypeStruct(v.shape, v.dtype) for v in (a, b)],
        compiler_params=pltpu.CompilerParams(vmem_limit_bytes=60 * 1024 * 1024),
    )(a, b)


def on_device(n_row, n_depth, n_col, inputs, cotangent, w_in, w_out):
    width = w_in.shape[0]
    units = w_in.shape[1] // n_depth
    block = inputs.shape[0]
    n_plane = n_depth * n_col
    tokens = block * n_plane
    part = width // n_depth
    n_chunks = units // UNITS
    quarter = tokens // 4
    nz = n_row // 2
    slots, stages = nz + 3, 3
    dma, regular = pltpu.SemaphoreType.DMA, pltpu.SemaphoreType.REGULAR
    vmem, hbm = pl.BlockSpec(memory_space=pltpu.VMEM), pl.BlockSpec(memory_space=pl.ANY)
    outputs, grad_inputs, grad_w_in, grad_w_out = pl.pallas_call(
        functools.partial(kernel, n_row, n_depth, n_col),
        out_shape=(
            jax.ShapeDtypeStruct((block, width), BF16),
            jax.ShapeDtypeStruct((block, width), BF16),
            jax.ShapeDtypeStruct((width, units), BF16),
            jax.ShapeDtypeStruct((w_out.shape[0], part), BF16),
        ),
        in_specs=[vmem] * 2 + [hbm] * 2,
        out_specs=(vmem, vmem, hbm, hbm),
        scratch_shapes=[
            pltpu.VMEM((tokens, width), BF16),
            pltpu.VMEM((width, tokens), BF16),
            pltpu.VMEM((tokens, width), BF16),
            pltpu.VMEM((tokens, width), BF16),
            pltpu.VMEM((2, tokens, width), BF16),
            pltpu.VMEM((2, n_plane - 1, block, width), BF16),
            pltpu.VMEM((n_chunks, width, UNITS), BF16),
            pltpu.VMEM((n_chunks, UNITS, width), BF16),
            pltpu.VMEM((tokens, width), F32),
            pltpu.VMEM((tokens, width), F32),
            pltpu.VMEM((2, 2, 2, quarter, UNITS), BF16),
            pltpu.VMEM((2, 2, quarter, UNITS), BF16),
            pltpu.VMEM((nz, 2, quarter, UNITS), F32),
            pltpu.VMEM((slots, 2, quarter, UNITS), BF16),
            pltpu.VMEM((slots, 2, quarter, UNITS), BF16),
            pltpu.VMEM((stages, 2, quarter, UNITS), BF16),
            pltpu.VMEM((stages, 2, quarter, UNITS), BF16),
            pltpu.VMEM((2, 2, tokens, UNITS), BF16),
            pltpu.VMEM((2, width, UNITS), BF16),
            pltpu.VMEM((2, UNITS, part), BF16),
            pltpu.VMEM((2, UNITS, part), BF16),
            dma((n_chunks, 2)),
            dma((2, 2)), dma((2, 2)), regular((2,)),
            dma((stages, 2)), dma((slots, 2)), regular((2,)),
            dma((stages, 2)), dma((slots, 2)), regular((2,)),
            dma((2, 2, 2)), dma((2, 2, 2)), regular((2,)),
            dma((2,)), dma((2,)), dma((2,)), dma((n_chunks,)),
            dma((2, n_plane - 1)), dma((2, n_plane - 1)), dma((2, n_plane - 1)), dma((2, n_plane - 1)),
        ],
        compiler_params=pltpu.CompilerParams(
            collective_id=0, has_side_effects=True, vmem_limit_bytes=60 * 1024 * 1024
        ),
        cost_estimate=pl.CostEstimate(
            flops=12 * tokens * width * units, bytes_accessed=6 * width * units * 2,
            transcendentals=tokens * units,
        ),
    )(inputs, cotangent, w_in, w_out)
    grad_w_in, grad_w_out = copied(grad_w_in, grad_w_out)
    return (outputs, grad_inputs, grad_w_in, grad_w_out)


def solution(mesh):
    in_specs = (
        P(("depth", "col"), "row"),
        P(("depth", "col"), "row"),
        P("row", "col"),
        P("col", "row"),
    )
    out_specs = (
        P(("depth", "col"), "row"),
        P(("depth", "col"), "row"),
        P("row", ("col", "depth")),
        P("col", ("row", "depth")),
    )
    return jax.shard_map(
        functools.partial(on_device, *(mesh.shape[a] for a in ("row", "depth", "col"))),
        mesh=mesh, in_specs=in_specs, out_specs=out_specs, check_vma=False,
    )
```
